128 devices in a mesh: pb: 16 (over z, x_lo, core), tile: 8 (over x_hi, y).
Axes of the slice: x: 4 (x_hi: 2, x_lo: 2; x = x_hi * 2 + x_lo), y: 4, z: 4, core: 2. Of those that a mesh axis runs over, the one named last changes fastest.
Arguments:
- trials: bfloat16 [16, 4, 4096], P('pb', None, 'tile'), may hold values from -6 to 6
- w_screen: bfloat16 [16, 2048, 2048], P('pb', 'tile'), may hold values from -48 to 48
- cond_bands: bfloat16 [16, 2048, 64], P('pb', 'tile'), may hold values from -0.125 to 0.125
- val_bands: bfloat16 [16, 2048, 64], P('pb', 'tile'), may hold values from -0.125 to 0.125
- pair_table: int32 [16, 16], replicated, may hold values from 0 to 15, as said below
Outputs:
- applied: bfloat16 [16, 4, 4096], P('pb', None, 'tile')
The draws below stay inside these ranges and needn't reach their ends.
Inputs may be any that keep to these rules, and one draw needn't show every extreme that they name: Every row and every column of pair_table holds each k-point exactly once.
All inputs are finite; a program needn't handle non-finite values.
Results may differ from the reference program's by a relative error of at most 0.023.
Values may be sent and summed in bfloat16 or wider, within the bound.
A program may use at most 128 MiB of HBM per device.

```python
import jax
import jax.numpy as jnp
from jax import lax

NK = 16
NS = 4
NP = 2048
NC = 64
NV = 64


def draw_pair_table(key, part):
    labels = jax.random.permutation(jax.random.fold_in(key, 7), NK)
    places = jnp.argsort(labels)
    differ = (places[:, None] - places[None, :]) % NK
    return labels[differ].astype(jnp.int32)


def levels(rng, extent, pieces, least, largest):
    gain, own = 1.0, jax.random.fold_in(rng, 6)
    for axis_at, blocks in pieces:
        draws = jnp.exp(jax.random.uniform(jax.random.fold_in(own, axis_at), (blocks,), jnp.float32, least / len(pieces), largest / len(pieces)))
        gain = gain * jnp.repeat(draws, extent[axis_at] // blocks).reshape([-1 if axis == axis_at else 1 for axis in range(len(extent))])
    return gain


def bell_draw(key, dims, deviation, limit, split=(), kind=jnp.bfloat16):
    level = levels(key, dims, split, -0.22, 0.18) if split else 1.0
    entries = jax.random.normal(key, dims, jnp.float32) * deviation * level
    return jnp.minimum(jnp.maximum(entries, -limit), limit).astype(kind)


def setup_inputs(seed: int = 0) -> dict:
    streams_of = jax.random.split(jax.random.key(seed), 6)
    return {
        "trials": bell_draw(streams_of[0], (NK, NS, NC * NV), 1.0, 6.0, ((0, 16), (2, 8))),
        "w_screen": bell_draw(streams_of[1], (NK, NP, NP), 8.0, 48.0, ((0, 16), (1, 8))),
        "cond_bands": bell_draw(streams_of[2], (NK, NP, NC), NP ** -0.5, 0.125, ((0, 16), (1, 8))),
        "val_bands": bell_draw(streams_of[3], (NK, NP, NV), NP ** -0.5, 0.125, ((0, 16), (1, 8))),
        "pair_table": draw_pair_table(jax.random.fold_in(streams_of[5], 71), 0),
    }


def reference(trials, w_screen, cond_bands, val_bands, pair_table):
    xmat = trials.reshape(NK, NS, NC, NV).astype(jnp.float32)
    cond_all = cond_bands.astype(jnp.float32)
    val_all = val_bands.astype(jnp.float32)
    amat = jnp.einsum('kpc,kscv->kspv', cond_all, xmat).astype(jnp.bfloat16)

    def one_pair(carry, index):
        qpoint = index // NK
        kpoint = index % NK
        kprime = pair_table[kpoint, qpoint]
        mmat = jnp.einsum('spv,nv->spn', amat[kprime].astype(jnp.float32), val_all[kprime])
        pmat = (mmat * w_screen[qpoint].astype(jnp.float32)).astype(jnp.bfloat16).astype(jnp.float32)
        gmat = jnp.einsum('pc,spn->scn', cond_all[kpoint], pmat).astype(jnp.bfloat16).astype(jnp.float32)
        contrib = jnp.einsum('scn,nv->scv', gmat, val_all[kpoint])
        return carry.at[kpoint].add(contrib), None

    start = jnp.zeros((NK, NS, NC, NV), jnp.float32)
    total, unused = lax.scan(one_pair, start, jnp.arange(NK * NK, dtype=jnp.int32))
    return total.reshape(NK, NS, NC * NV).astype(jnp.bfloat16)
```

```python
import jax
import jax.numpy as jnp
from jax import lax
from jax.experimental import pallas as pl
from jax.experimental.pallas import tpu as pltpu
from jax.sharding import PartitionSpec as P

MESH = pl.DeviceIdType.MESH
bf16 = jnp.bfloat16
f32 = jnp.float32
NN = (((1,), (0,)), ((), ()))
NT = (((1,), (1,)), ((), ()))
TN = (((0,), (0,)), ((), ()))

OWN_X, OWN_UP, OWN_DN, OWN_SIB = 0, 1, 2, 3
XC_UP, XC_DN, XC_SIB = 4, 5, 6
FAR_UP, FAR_DN = (7, 8), (9, 10)
DN_SIB, UP_SIB, FAR_SIB = (11, 12), (13, 14), (15, 16)
KINDS = 17


def dot(a, b, dims):
    return lax.dot_general(a, b, dims, preferred_element_type=f32)


def kernel(
    x_ref, w_ref, ucin_ref, uvin_ref, tab_ref, out_ref,
    uv, xb, uc, p0, p1, a0, a1, g, yout, yin, y2out, y2in, xs, os,
    tsend, trecv, ucsend, ucrecv, isend, irecv, ysend, yrecv, zsend, zrecv,
):
    q = lax.axis_index("pb")
    t = lax.axis_index("tile")
    z, h, c = q // 4, (q // 2) % 2, q % 2

    def kof(dz, dh, dc):
        return ((z + dz) % 4) * 4 + ((h + dh) % 2) * 2 + (c + dc) % 2

    me = kof(0, 0, 0)

    barrier = pltpu.get_barrier_semaphore()
    for j in range(1, 16):
        pl.semaphore_signal(barrier, inc=1, device_id=((q + j) % 16, t), device_id_type=MESH)
    for j in range(1, 8):
        pl.semaphore_signal(barrier, inc=1, device_id=(q, (t + j) % 8), device_id_type=MESH)

    uv[me, t] = jnp.transpose(uvin_ref[0].astype(f32)).astype(bf16)
    uc[z, q % 4] = jnp.transpose(ucin_ref[0].astype(f32)).astype(bf16)
    xin = x_ref[0].astype(f32)
    for s in range(4):
        for b in range(8):
            xs[(s // 2) * 8 + b : (s // 2) * 8 + b + 1, (s % 2) * 64 : (s % 2) * 64 + 64] = xin[
                s : s + 1, b * 64 : b * 64 + 64
            ]
    xb[me, t] = xs[...].astype(bf16)

    pl.semaphore_wait(barrier, 22)

    def remote(src, dst, ssem, rsem, pb, tile):
        return pltpu.make_async_remote_copy(
            src_ref=src, dst_ref=dst, send_sem=ssem, recv_sem=rsem,
            device_id=(pb, tile), device_id_type=MESH,
        )

    def tcopy(j, owner, peer):
        return (
            remote(uv.at[me, owner], uv.at[me, owner], tsend.at[0, j], trecv.at[0, j], q, peer),
            remote(xb.at[me, owner], xb.at[me, owner], tsend.at[1, j], trecv.at[1, j], q, peer),
        )

    def ccopy(j, owner_z, peer):
        blk = uc.at[owner_z, q % 4]
        return remote(blk, blk, ucsend.at[j], ucrecv.at[j], peer, t)

    def ccolumn(j, dh, dc, peer):
        blk = uc.at[:, kof(0, dh, dc) % 4]
        return remote(blk, blk, ucsend.at[j], ucrecv.at[j], peer, t)

    sib, xnb, up, dn = kof(0, 0, 1), kof(0, 1, 0), kof(1, 0, 0), kof(3, 0, 0)

    for j in range(1, 8):
        for copy in tcopy(j, t, (t + j) % 8):
            copy.start()
    for j in range(1, 4):
        ccopy(j, z, kof(j, 0, 0)).start()
    for j in range(1, 4):
        ccopy(j, (z - j + 4) % 4, q).wait_recv()
    ccolumn(4, 0, 0, xnb).start()
    ccolumn(5, 0, 0, sib).start()

    def record(kind, k, peer, part=None):
        at = (k,) if part is None else (k, pl.ds(part * 4, 4))
        return (
            remote(uv.at[at], uv.at[at], isend.at[0, kind], irecv.at[0, kind], peer, t),
            remote(xb.at[at], xb.at[at], isend.at[1, kind], irecv.at[1, kind], peer, t),
        )

    def send(*args):
        for copy in record(*args):
            copy.start()

    def take(*args):
        for copy in record(*args):
            copy.wait_recv()

    def boundary_0():
        for j in range(1, 8):
            for copy in tcopy(j, (t - j + 8) % 8, t):
                copy.wait_recv()
        send(OWN_SIB, me, sib)
        send(OWN_X, me, xnb)
        send(OWN_UP, me, up)
        send(OWN_DN, me, dn)

    def boundary_1():
        take(OWN_SIB, kof(0, 0, 1), q)

    def boundary_2():
        k = kof(0, 1, 0)
        take(OWN_X, k, q)
        send(XC_SIB, k, sib)
        send(XC_UP, k, up)
        send(XC_DN, k, dn)

    def pass_on(dh, from_dn, from_up):
        k = kof(3, dh, 0)
        take(from_dn, k, q)
        send(DN_SIB[dh], k, sib)
        send(FAR_UP[dh], k, up, 0)
        k = kof(1, dh, 0)
        take(from_up, k, q)
        send(UP_SIB[dh], k, sib)
        send(FAR_DN[dh], k, dn, 1)

    def boundary_3():
        take(XC_SIB, kof(0, 1, 1), q)
        pass_on(0, OWN_UP, OWN_DN)

    def boundary_5():
        take(DN_SIB[0], kof(3, 0, 1), q)

    def boundary_6():
        pass_on(1, XC_UP, XC_DN)

    def far(dh):
        k = kof(2, dh, 0)
        take(FAR_UP[dh], k, q, 0)
        take(FAR_DN[dh], k, q, 1)
        send(FAR_SIB[dh], k, sib)

    def boundary_7():
        take(UP_SIB[0], kof(1, 0, 1), q)

    def boundary_8():
        far(0)

    def boundary_9():
        take(DN_SIB[1], kof(3, 1, 1), q)

    def boundary_10():
        far(1)

    def boundary_11():
        take(UP_SIB[1], kof(1, 1, 1), q)

    def boundary_13():
        take(FAR_SIB[0], kof(2, 0, 1), q)

    def boundary_15():
        take(FAR_SIB[1], kof(2, 1, 1), q)

    def item(b2, dc):
        dz = jnp.where(b2 < 2, 0, jnp.where(b2 >= 6, 2, jnp.where(b2 % 2 == 0, 3, 1)))
        dh = jnp.where(b2 < 2, b2, jnp.where(b2 < 4, 0, jnp.where(b2 < 6, 1, b2 - 6)))
        return kof(dz, dh, dc)

    def amat(k, a):
        u = uc[k // 4, k % 4]
        xk = xb[k].astype(f32)
        for sh in range(2):
            xm = xk[:, sh * 8 : sh * 8 + 8, :].reshape(64, 128).astype(bf16)
            both = dot(u, xm, TN).astype(bf16)
            a[2 * sh] = both[:, :64]
            a[2 * sh + 1] = both[:, 64:]

    def pmat(k, a, p, b):
        n = slice(b * 256, b * 256 + 256)
        wb = w_ref[0, :, n].astype(f32)
        for s in range(4):
            p[s, :, n] = (dot(a[s], uv[k, b], NN) * wb).astype(bf16)

    def partner(kp):
        k = jnp.int32(0)
        for i in range(1, 16):
            k = jnp.where(tab_ref[i, q] == kp, i, k)
        return k

    def gmat(u, kp, p, b):
        n = slice(b * 256, b * 256 + 256)
        for s in range(4):
            g[kp, s * 64 : s * 64 + 64, n] = dot(u, p[s, :, n], NN).astype(bf16)

    def half(b2, dc, b2n, dcn, pr, pw, an):
        kp, kn = item(b2, dc), item(b2n, dcn)
        kk = partner(kp)
        u = uc[kk // 4, kk % 4]
        amat(kn, an)
        for b in range(8):
            gmat(u, kp, pr, b)
            pmat(kn, an, pw, b)

    boundary_0()
    amat(me, a0)
    for b in range(8):
        pmat(me, a0, p0, b)
    ccolumn(4, 1, 0, q).wait_recv()
    ccolumn(6, 1, 0, sib).start()
    ccolumn(5, 0, 1, q).wait_recv()
    ccolumn(6, 1, 1, q).wait_recv()

    odd = {1: boundary_1, 3: boundary_3, 5: boundary_5, 7: boundary_7, 9: boundary_9, 11: boundary_11, 13: boundary_13}
    even = {2: boundary_2, 6: boundary_6, 8: boundary_8, 10: boundary_10}

    def body(j, carry):
        for b, act in odd.items():
            pl.when(2 * j + 1 == b)(act)
        half(j, 0, j, 1, p0, p1, a1)
        for b, act in even.items():
            pl.when(2 * j + 2 == b)(act)
        half(j, 1, j + 1, 0, p1, p0, a0)
        return carry

    lax.fori_loop(0, 7, body, 0)
    boundary_15()
    half(7, 0, 7, 1, p0, p1, a1)
    last = item(7, 1)
    kk = partner(last)
    u = uc[kk // 4, kk % 4]
    for b in range(8):
        gmat(u, last, p1, b)

    def ycopy(j, owner, k, peer):
        return remote(yout.at[k], yin.at[owner], ysend.at[j], yrecv.at[j], peer, t)

    def ymat(k):
        kp = tab_ref[k, q]
        acc = jnp.zeros((256, 64), f32)
        for b in range(8):
            acc = acc + dot(g[kp, :, b * 256 : b * 256 + 256], uv[k, b], NT)
        both = jnp.concatenate([acc[:128], acc[128:]], axis=1)
        return jnp.swapaxes(both.reshape(2, 8, 8, 128), 0, 1).reshape(8, 16, 128)

    def ybody(j, carry):
        k = (q + j) % 16
        yout[k] = ymat(k).astype(bf16)
        ycopy(j, q, k, k).start()
        return carry

    lax.fori_loop(1, 16, ybody, 0)
    total = ymat(q)
    for j in range(1, 16):
        owner = (q - j + 16) % 16
        ycopy(j, owner, q, q).wait_recv()
        total = total + yin[owner].astype(f32)
    y2out[...] = total.astype(bf16)

    def zcopy(j, owner, part, peer):
        return remote(y2out.at[part], y2in.at[owner], zsend.at[j], zrecv.at[j], q, peer)

    for j in range(1, 8):
        zcopy(j, t, (t + j) % 8, (t + j) % 8).start()
    res = y2out[t].astype(f32)
    for j in range(1, 8):
        owner = (t - j + 8) % 8
        zcopy(j, owner, t, t).wait_recv()
        res = res + y2in[owner].astype(f32)
    for s in range(4):
        for b in range(8):
            os[s : s + 1, b * 64 : b * 64 + 64] = res[
                (s % 2) * 8 + b : (s % 2) * 8 + b + 1, (s // 2) * 64 : (s // 2) * 64 + 64
            ]
    out_ref[0] = os[...].astype(bf16)

    for j in range(1, 8):
        for copy in tcopy(j, t, (t + j) % 8):
            copy.wait_send()
        zcopy(j, t, (t + j) % 8, (t + j) % 8).wait_send()
    for j in range(1, 4):
        ccopy(j, z, kof(j, 0, 0)).wait_send()
    ccolumn(4, 0, 0, xnb).wait_send()
    ccolumn(5, 0, 0, sib).wait_send()
    ccolumn(6, 1, 0, sib).wait_send()
    halves = {FAR_UP[0]: 0, FAR_UP[1]: 0, FAR_DN[0]: 1, FAR_DN[1]: 1}
    for kind in range(KINDS):
        for copy in record(kind, me, sib, halves.get(kind)):
            copy.wait_send()
    for j in range(1, 16):
        ycopy(j, q, (q + j) % 16, (q + j) % 16).wait_send()


def shards(trials, w_screen, cond_bands, val_bands, pair_table):
    vmem = pl.BlockSpec(memory_space=pltpu.VMEM)
    smem = pl.BlockSpec(memory_space=pltpu.SMEM)
    dma = pltpu.SemaphoreType.DMA
    return pl.pallas_call(
        kernel,
        out_shape=jax.ShapeDtypeStruct(trials.shape, bf16),
        in_specs=[vmem, vmem, vmem, vmem, smem],
        out_specs=vmem,
        scratch_shapes=[
            pltpu.VMEM((16, 8, 64, 256), bf16),
            pltpu.VMEM((16, 8, 16, 128), bf16),
            pltpu.VMEM((4, 4, 64, 256), bf16),
            pltpu.VMEM((4, 256, 2048), bf16),
            pltpu.VMEM((4, 256, 2048), bf16),
            pltpu.VMEM((4, 256, 64), bf16),
            pltpu.VMEM((4, 256, 64), bf16),
            pltpu.VMEM((16, 256, 2048), bf16),
            pltpu.VMEM((16, 8, 16, 128), bf16),
            pltpu.VMEM((16, 8, 16, 128), bf16),
            pltpu.VMEM((8, 16, 128), bf16),
            pltpu.VMEM((8, 16, 128), bf16),
            pltpu.VMEM((16, 128), f32),
            pltpu.VMEM((4, 512), f32),
            dma((2, 8)), dma((2, 8)),
            dma((8,)), dma((8,)),
            dma((2, KINDS)), dma((2, KINDS)),
            dma((16,)), dma((16,)),
            dma((8,)), dma((8,)),
        ],
        compiler_params=pltpu.CompilerParams(
            collective_id=0, has_side_effects=True, vmem_limit_bytes=50 * 2**20
        ),
    )(trials, w_screen, cond_bands, val_bands, pair_table)


def solution(mesh):
    in_specs = (
        P("pb", None, "tile"),
        P("pb", "tile", None),
        P("pb", "tile", None),
        P("pb", "tile", None),
        P(),
    )
    out_specs = P("pb", None, "tile")
    return jax.shard_map(shards, mesh=mesh, in_specs=in_specs, out_specs=out_specs, check_vma=False)
```

```python
import jax
import jax.numpy as jnp
from jax import lax
from jax.experimental import pallas as pl
from jax.experimental.pallas import tpu as pltpu
from jax.sharding import PartitionSpec as P

MESH = pl.DeviceIdType.MESH
bf16 = jnp.bfloat16
f32 = jnp.float32
NN = (((1,), (0,)), ((), ()))
NT = (((1,), (1,)), ((), ()))
TN = (((0,), (0,)), ((), ()))

OWN_X, OWN_UP, OWN_DN, OWN_SIB = (0, 1), (2, 3), (4, 5), (6, 7)
XC_UP, XC_DN, XC_SIB = (8, 9), (10, 11), (12, 13)
FAR_UP, FAR_DN = (14, 15), (16, 17)
DN_SIB, UP_SIB, FAR_SIB = (18, 19), (20, 21), (22, 23)
KINDS = 24
VMEM_LIMIT = 64 * 2**20 - 2**16
WHOLE = (18, 19, 20, 21, 22, 23)


def dot(a, b, dims):
    return lax.dot_general(a, b, dims, preferred_element_type=f32)


def kernel(
    x_hbm, w_hbm, uc_hbm, uv_hbm, tab_hbm, out_ref,
    x_ref, w_ref, tab_ref, uv, xb, uc, p0, p1, a0, a1, g, ysout, ysin, yout, yin, xs, os,
    lsem, tsend, trecv, ucsend, ucrecv, isend, irecv, ssend, srecv, ysend, yrecv,
):
    q = lax.axis_index("pb")
    t = lax.axis_index("tile")
    z, h, c = q // 4, (q // 2) % 2, q % 2
    hi, y = t // 4, t % 4

    def kof(dz, dh, dc):
        return ((z + dz) % 4) * 4 + ((h + dh) % 2) * 2 + (c + dc) % 2

    me = kof(0, 0, 0)
    local = (
        pltpu.make_async_copy(x_hbm.at[0], x_ref, lsem.at[0]),
        pltpu.make_async_copy(uv_hbm.at[0], uv.at[me, t], lsem.at[1]),
        pltpu.make_async_copy(uc_hbm.at[0], uc.at[z, q % 4], lsem.at[2]),
        pltpu.make_async_copy(w_hbm.at[0], w_ref, lsem.at[3]),
        pltpu.make_async_copy(tab_hbm, tab_ref, lsem.at[4]),
    )
    for copy in local:
        copy.start()

    barrier = pltpu.get_barrier_semaphore()
    for j in range(1, 8):
        pl.semaphore_signal(barrier, inc=1, device_id=(q, (t + j) % 8), device_id_type=MESH)
    for j in range(1, 16):
        pl.semaphore_signal(barrier, inc=1, device_id=((q + j) % 16, t), device_id_type=MESH)

    local[0].wait()
    xin = x_ref[...].astype(f32)
    for s in range(4):
        for b in range(8):
            xs[(s // 2) * 8 + b : (s // 2) * 8 + b + 1, (s % 2) * 64 : (s % 2) * 64 + 64] = xin[
                s : s + 1, b * 64 : b * 64 + 64
            ]
    xb[me, t] = xs[...].astype(bf16)
    local[1].wait()
    local[2].wait()

    pl.semaphore_wait(barrier, 22)

    def remote(src, dst, ssem, rsem, pb, tile):
        return pltpu.make_async_remote_copy(
            src_ref=src, dst_ref=dst, send_sem=ssem, recv_sem=rsem,
            device_id=(pb, tile), device_id_type=MESH,
        )

    def at_offset(j, sign):
        return ((hi + j // 4) % 2) * 4 + (y + sign * (j % 4) + 4) % 4

    def tcopy(j, owner, peer):
        return (
            remote(xb.at[me, owner], xb.at[me, owner], tsend.at[1, j], trecv.at[1, j], q, peer),
            remote(uv.at[me, owner], uv.at[me, owner], tsend.at[0, j], trecv.at[0, j], q, peer),
        )

    def ccopy(kind, dz, dh, dc, peer):
        blk = uc.at[(z + dz) % 4, kof(0, dh, dc) % 4]
        return remote(blk, blk, ucsend.at[kind], ucrecv.at[kind], peer, t)

    sib, xnb, up, dn = kof(0, 0, 1), kof(0, 1, 0), kof(1, 0, 0), kof(3, 0, 0)

    def spread(dz):
        ccopy(4 + dz, dz, 0, 0, xnb).start()
        ccopy(8 + dz, dz, 0, 0, sib).start()

    def record(kind, k, peer, first=None):
        at = (k,) if first is None else (k, pl.ds(first * 4, 4))
        return (
            remote(xb.at[at], xb.at[at], isend.at[1, kind], irecv.at[1, kind], peer, t),
            remote(uv.at[at], uv.at[at], isend.at[0, kind], irecv.at[0, kind], peer, t),
        )

    def send(*args):
        for copy in record(*args):
            copy.start()

    def take(*args):
        for copy in record(*args):
            copy.wait_recv()

    def part(i):
        return (hi + i) % 2

    def send_own(i):
        send(OWN_X[i], me, xnb, part(i))
        send(OWN_UP[i], me, up, part(i))
        send(OWN_DN[i], me, dn, part(i))
        send(OWN_SIB[i], me, sib, part(i))

    def x_item(i):
        k = kof(0, 1, 0)
        take(OWN_X[i], k, q, part(i))
        send(XC_UP[i], k, up, part(i))
        send(XC_DN[i], k, dn, part(i))
        send(XC_SIB[i], k, sib, part(i))

    def pass_on(dh, from_dn, from_up):
        k = kof(3, dh, 0)
        for i in range(2):
            take(from_dn[i], k, q, part(i))
        send(FAR_UP[dh], k, up, 0)
        send(DN_SIB[dh], k, sib)
        k = kof(1, dh, 0)
        for i in range(2):
            take(from_up[i], k, q, part(i))
        send(FAR_DN[dh], k, dn, 1)
        send(UP_SIB[dh], k, sib)

    def boundary_3():
        for i in range(2):
            take(XC_SIB[i], kof(0, 1, 1), q, part(i))

    def boundary_5():
        take(DN_SIB[0], kof(3, 0, 1), q)

    def boundary_6():
        pass_on(1, XC_UP, XC_DN)

    def far(dh):
        k = kof(2, dh, 0)
        take(FAR_UP[dh], k, q, 0)
        take(FAR_DN[dh], k, q, 1)
        send(FAR_SIB[dh], k, sib)

    def boundary_7():
        take(UP_SIB[0], kof(1, 0, 1), q)

    def boundary_8():
        far(0)

    def boundary_9():
        take(DN_SIB[1], kof(3, 1, 1), q)

    def boundary_10():
        far(1)

    def boundary_11():
        take(UP_SIB[1], kof(1, 1, 1), q)

    def boundary_13():
        take(FAR_SIB[0], kof(2, 0, 1), q)

    def boundary_15():
        take(FAR_SIB[1], kof(2, 1, 1), q)

    def item(b2, dc):
        dz = jnp.where(b2 < 2, 0, jnp.where(b2 >= 6, 2, jnp.where(b2 % 2 == 0, 3, 1)))
        dh = jnp.where(b2 < 2, b2, jnp.where(b2 < 4, 0, jnp.where(b2 < 6, 1, b2 - 6)))
        return kof(dz, dh, dc)

    def amat(k, a):
        u = uc[k // 4, k % 4]
        xk = xb[k].astype(f32)
        for sh in range(2):
            xm = xk[:, sh * 8 : sh * 8 + 8, :].reshape(64, 128).astype(bf16)
            both = dot(u, xm, TN).astype(bf16)
            a[2 * sh] = both[:, :64]
            a[2 * sh + 1] = both[:, 64:]

    def pmat(k, a, p, b):
        n = slice(b * 256, b * 256 + 256)
        wb = w_ref[:, n].astype(f32)
        for s in range(4):
            p[s, :, n] = (dot(a[s], uv[k, b], NN) * wb).astype(bf16)

    def partner(kp):
        k = jnp.int32(0)
        for i in range(1, 16):
            k = jnp.where(tab_ref[i, q] == kp, i, k)
        return k

    def gmat(u, kp, p, b):
        n = slice(b * 256, b * 256 + 256)
        for s in range(4):
            g[kp, s * 64 : s * 64 + 64, n] = dot(u, p[s, :, n], NN).astype(bf16)

    def half(b2, dc, b2n, dcn, pr, pw, an):
        kp, kn = item(b2, dc), item(b2n, dcn)
        kk = partner(kp)
        u = uc[kk // 4, kk % 4]
        amat(kn, an)
        for b in range(8):
            gmat(u, kp, pr, b)
            pmat(kn, an, pw, b)

    def gmat_all(b2, dc, p):
        kp = item(b2, dc)
        kk = partner(kp)
        u = uc[kk // 4, kk % 4]
        for b in range(8):
            gmat(u, kp, p, b)

    def pmat_all(b2, dc, a, p):
        k = item(b2, dc)
        amat(k, a)
        for b in range(8):
            pmat(k, a, p, b)

    for j in range(1, 4):
        ccopy(j, 0, 0, 0, kof(j, 0, 0)).start()
    for j in (6, 5, 7, 4, 2, 1, 3):
        for copy in tcopy(j, t, at_offset(j, 1)):
            copy.start()
    spread(0)
    for j in (1, 3):
        ccopy(j, 4 - j, 0, 0, q).wait_recv()
        spread(4 - j)
    for j in range(1, 4):
        for copy in tcopy(j, at_offset(j, -1), t):
            copy.wait_recv()
    send_own(0)
    ccopy(2, 2, 0, 0, q).wait_recv()
    spread(2)
    for j in range(4, 8):
        for copy in tcopy(j, at_offset(j, -1), t):
            copy.wait_recv()
    send_own(1)
    for j in (0, 1, 3, 2):
        ccopy(4 + j, j, 1, 0, q).wait_recv()
        ccopy(12 + j, j, 1, 0, sib).start()
    local[3].wait()
    local[4].wait()
    pmat_all(0, 0, a0, p0)
    x_item(0)
    for i in range(2):
        take(OWN_SIB[i], kof(0, 0, 1), q, part(i))
    for j in range(4):
        ccopy(8 + j, j, 0, 1, q).wait_recv()
        ccopy(12 + j, j, 1, 1, q).wait_recv()
    pmat_all(0, 1, a1, p1)
    gmat_all(0, 0, p0)
    x_item(1)
    gmat_all(0, 1, p1)
    pass_on(0, OWN_UP, OWN_DN)
    pmat_all(1, 0, a0, p0)

    odd = {3: boundary_3, 5: boundary_5, 7: boundary_7, 9: boundary_9, 11: boundary_11, 13: boundary_13}
    even = {6: boundary_6, 8: boundary_8, 10: boundary_10}

    def body(j, carry):
        for b, act in odd.items():
            pl.when(2 * j + 3 == b)(act)
        half(j + 1, 0, j + 1, 1, p0, p1, a1)
        for b, act in even.items():
            pl.when(2 * j + 4 == b)(act)
        half(j + 1, 1, j + 2, 0, p1, p0, a0)
        return carry

    lax.fori_loop(0, 6, body, 0)
    boundary_15()
    half(7, 0, 7, 1, p0, p1, a1)
    gmat_all(7, 1, p1)

    def ymat(k):
        kp = tab_ref[k, q]
        acc = jnp.zeros((256, 64), f32)
        for b in range(8):
            acc = acc + dot(g[kp, :, b * 256 : b * 256 + 256], uv[k, b], NT)
        both = jnp.concatenate([acc[:128], acc[128:]], axis=1)
        return jnp.swapaxes(both.reshape(2, 8, 8, 128), 0, 1).reshape(8, 16, 128)

    chip = q // 2

    def scopy(m):
        return remote(ysout.at[m], ysin.at[m], ssend.at[m], srecv.at[m], sib, t)

    def to_sibling(j, carry):
        m = (chip + j) % 8
        ysout[m] = ymat(m * 2 + 1 - c).astype(bf16)
        scopy(m).start()
        return carry

    lax.fori_loop(1, 9, to_sibling, 0)

    def ycopy(j, m, owner, peer):
        return remote(yout.at[m, peer], yin.at[chip, owner], ysend.at[j], yrecv.at[j], m * 2 + c, peer)

    own = pltpu.make_async_copy(yout.at[chip, t], yin.at[chip, t], yrecv.at[0])

    def to_owners(j, carry):
        m = (chip + j) % 8
        part_sum = ymat(m * 2 + c)
        scopy(m).wait_recv()
        yout[m] = (part_sum + ysin[m].astype(f32)).astype(bf16)
        for i in range(8):
            ycopy(j, m, t, (t + i) % 8).start()
        return carry

    lax.fori_loop(1, 8, to_owners, 0)
    part_sum = ymat(q)
    scopy(chip).wait_recv()
    yout[chip] = (part_sum + ysin[chip].astype(f32)).astype(bf16)
    for i in range(1, 8):
        ycopy(0, chip, t, (t + i) % 8).start()
    own.start()

    res = jnp.zeros((16, 128), f32)
    for j in (1, 2, 3, 4, 5, 6, 7, 0):
        m = (chip - j + 8) % 8
        pltpu.make_async_copy(yin.at[m], yin.at[m], yrecv.at[j]).wait()
        res = res + jnp.sum(yin[m].astype(f32), axis=0)
    for s in range(4):
        for b in range(8):
            os[s : s + 1, b * 64 : b * 64 + 64] = res[
                (s % 2) * 8 + b : (s % 2) * 8 + b + 1, (s // 2) * 64 : (s // 2) * 64 + 64
            ]
    out_ref[0] = os[...].astype(bf16)

    for j in range(1, 8):
        for copy in tcopy(j, t, at_offset(j, 1)):
            copy.wait_send()
        pltpu.make_async_copy(yout.at[j], yout.at[j], ysend.at[j]).wait()
    pltpu.make_async_copy(yout.at[0, pl.ds(0, 7)], yout.at[0, pl.ds(0, 7)], ysend.at[0]).wait()
    for j in range(8):
        scopy(j).wait_send()
    for j in range(1, 16):
        ccopy(j, 0, 0, 0, sib).wait_send()
    for kind in range(KINDS):
        for copy in record(kind, me, sib, None if kind in WHOLE else 0):
            copy.wait_send()


def shards(trials, w_screen, cond_bands, val_bands, pair_table):
    vmem = pl.BlockSpec(memory_space=pltpu.VMEM)
    hbm = pl.BlockSpec(memory_space=pltpu.HBM)
    dma = pltpu.SemaphoreType.DMA
    return pl.pallas_call(
        kernel,
        out_shape=jax.ShapeDtypeStruct(trials.shape, bf16),
        in_specs=[hbm] * 5,
        out_specs=vmem,
        scratch_shapes=[
            pltpu.VMEM((4, 512), bf16),
            pltpu.VMEM((256, 2048), bf16),
            pltpu.SMEM((16, 16), jnp.int32),
            pltpu.VMEM((16, 8, 64, 256), bf16),
            pltpu.VMEM((16, 8, 16, 128), bf16),
            pltpu.VMEM((4, 4, 64, 256), bf16),
            pltpu.VMEM((4, 256, 2048), bf16),
            pltpu.VMEM((4, 256, 2048), bf16),
            pltpu.VMEM((4, 256, 64), bf16),
            pltpu.VMEM((4, 256, 64), bf16),
            pltpu.VMEM((16, 256, 2048), bf16),
            pltpu.VMEM((8, 8, 16, 128), bf16),
            pltpu.VMEM((8, 8, 16, 128), bf16),
            pltpu.VMEM((8, 8, 16, 128), bf16),
            pltpu.VMEM((8, 8, 16, 128), bf16),
            pltpu.VMEM((16, 128), f32),
            pltpu.VMEM((4, 512), f32),
            dma((5,)),
            dma((2, 8)), dma((2, 8)),
            dma((16,)), dma((16,)),
            dma((2, KINDS)), dma((2, KINDS)),
            dma((8,)), dma((8,)),
            dma((8,)), dma((8,)),
        ],
        compiler_params=pltpu.CompilerParams(
            collective_id=0, has_side_effects=True, vmem_limit_bytes=VMEM_LIMIT
        ),
    )(trials, w_screen, jnp.swapaxes(cond_bands, 1, 2), jnp.swapaxes(val_bands, 1, 2), pair_table)


def solution(mesh):
    in_specs = (
        P("pb", None, "tile"),
        P("pb", "tile", None),
        P("pb", "tile", None),
        P("pb", "tile", None),
        P(),
    )
    out_specs = P("pb", None, "tile")
    return jax.shard_map(shards, mesh=mesh, in_specs=in_specs, out_specs=out_specs, check_vma=False)
```

```python
import jax
import jax.numpy as jnp
from jax import lax
from jax.experimental import pallas as pl
from jax.experimental.pallas import tpu as pltpu
from jax.sharding import PartitionSpec as P

MESH = pl.DeviceIdType.MESH
bf16 = jnp.bfloat16
f32 = jnp.float32
NN = (((1,), (0,)), ((), ()))
NT = (((1,), (1,)), ((), ()))
TN = (((0,), (0,)), ((), ()))

OWN_X, OWN_UP, OWN_DN, OWN_SIB = (0, 1), (2, 3), (4, 5), (6, 7)
XC_UP, XC_DN, XC_SIB = (8, 9), (10, 11), (12, 13)
FAR_UP, FAR_DN = (14, 15), (16, 17)
DN_SIB, UP_SIB, FAR_SIB = (18, 19), (20, 21), (22, 23)
KINDS = 24
VMEM_LIMIT = 60 * 2**20
WHOLE = (18, 19, 20, 21, 22, 23)


def dot(a, b, dims):
    return lax.dot_general(a, b, dims, preferred_element_type=f32)


def kernel(
    x_hbm, w_hbm, uc_hbm, uv_hbm, tab_hbm, out_ref,
    x_ref, w_ref, tab_ref, uv, xb, uc, p0, p1, a0, a1, g, ysout, ysin, yout, yin, xs, os,
    lsem, tsend, trecv, ucsend, ucrecv, isend, irecv, ssend, srecv, ysend, yrecv,
):
    q = lax.axis_index("pb")
    t = lax.axis_index("tile")
    z, h, c = q // 4, (q // 2) % 2, q % 2
    hi, y = t // 4, t % 4

    def kof(dz, dh, dc):
        return ((z + dz) % 4) * 4 + ((h + dh) % 2) * 2 + (c + dc) % 2

    me = kof(0, 0, 0)
    local = (
        pltpu.make_async_copy(x_hbm.at[0], x_ref, lsem.at[0]),
        pltpu.make_async_copy(uv_hbm.at[0], uv.at[me, t], lsem.at[1]),
        pltpu.make_async_copy(uc_hbm.at[0], uc.at[z, q % 4], lsem.at[2]),
        pltpu.make_async_copy(w_hbm.at[0], w_ref, lsem.at[3]),
        pltpu.make_async_copy(tab_hbm, tab_ref, lsem.at[4]),
    )
    for copy in local:
        copy.start()

    barrier = pltpu.get_barrier_semaphore()
    for j in range(1, 8):
        pl.semaphore_signal(barrier, inc=1, device_id=(q, (t + j) % 8), device_id_type=MESH)
    for j in range(1, 16):
        pl.semaphore_signal(barrier, inc=1, device_id=((q + j) % 16, t), device_id_type=MESH)

    local[0].wait()
    xin = x_ref[...].astype(f32)
    for s in range(4):
        for b in range(8):
            xs[(s // 2) * 8 + b : (s // 2) * 8 + b + 1, (s % 2) * 64 : (s % 2) * 64 + 64] = xin[
                s : s + 1, b * 64 : b * 64 + 64
            ]
    xb[me, t] = xs[...].astype(bf16)
    local[1].wait()
    local[2].wait()

    pl.semaphore_wait(barrier, 22)

    def remote(src, dst, ssem, rsem, pb, tile):
        return pltpu.make_async_remote_copy(
            src_ref=src, dst_ref=dst, send_sem=ssem, recv_sem=rsem,
            device_id=(pb, tile), device_id_type=MESH,
        )

    def at_offset(j, sign):
        return ((hi + j // 4) % 2) * 4 + (y + sign * (j % 4) + 4) % 4

    def tcopy(j, owner, peer):
        return (
            remote(xb.at[me, owner], xb.at[me, owner], tsend.at[1, j], trecv.at[1, j], q, peer),
            remote(uv.at[me, owner], uv.at[me, owner], tsend.at[0, j], trecv.at[0, j], q, peer),
        )

    def ccopy(kind, dz, dh, dc, peer):
        blk = uc.at[(z + dz) % 4, kof(0, dh, dc) % 4]
        return remote(blk, blk, ucsend.at[kind], ucrecv.at[kind], peer, t)

    sib, xnb, up, dn = kof(0, 0, 1), kof(0, 1, 0), kof(1, 0, 0), kof(3, 0, 0)

    away = ((2, 1), (2, 0), (1, 1), (3, 1), (1, 0), (3, 0), (0, 1))

    def record(kind, k, peer, first=None):
        at = (k,) if first is None else (k, pl.ds(first * 4, 4))
        return (
            remote(xb.at[at], xb.at[at], isend.at[1, kind], irecv.at[1, kind], peer, t),
            remote(uv.at[at], uv.at[at], isend.at[0, kind], irecv.at[0, kind], peer, t),
        )

    def send(*args):
        for copy in record(*args):
            copy.start()

    def take(*args):
        for copy in record(*args):
            copy.wait_recv()

    def part(i):
        return (hi + i) % 2

    def send_own(i):
        send(OWN_X[i], me, xnb, part(i))
        send(OWN_UP[i], me, up, part(i))
        send(OWN_DN[i], me, dn, part(i))
        send(OWN_SIB[i], me, sib, part(i))

    def x_item(i):
        k = kof(0, 1, 0)
        take(OWN_X[i], k, q, part(i))
        send(XC_UP[i], k, up, part(i))
        send(XC_DN[i], k, dn, part(i))
        send(XC_SIB[i], k, sib, part(i))

    def pass_on(dh, from_dn, from_up):
        k = kof(3, dh, 0)
        for i in range(2):
            take(from_dn[i], k, q, part(i))
        send(FAR_UP[dh], k, up, 0)
        send(DN_SIB[dh], k, sib)
        k = kof(1, dh, 0)
        for i in range(2):
            take(from_up[i], k, q, part(i))
        send(FAR_DN[dh], k, dn, 1)
        send(UP_SIB[dh], k, sib)

    def boundary_3():
        for i in range(2):
            take(XC_SIB[i], kof(0, 1, 1), q, part(i))

    def boundary_5():
        take(DN_SIB[0], kof(3, 0, 1), q)

    def boundary_6():
        pass_on(1, XC_UP, XC_DN)

    def far(dh):
        k = kof(2, dh, 0)
        take(FAR_UP[dh], k, q, 0)
        take(FAR_DN[dh], k, q, 1)
        send(FAR_SIB[dh], k, sib)

    def boundary_7():
        take(UP_SIB[0], kof(1, 0, 1), q)

    def boundary_8():
        far(0)

    def boundary_9():
        take(DN_SIB[1], kof(3, 1, 1), q)

    def boundary_10():
        far(1)

    def boundary_11():
        take(UP_SIB[1], kof(1, 1, 1), q)

    def boundary_13():
        take(FAR_SIB[0], kof(2, 0, 1), q)

    def boundary_15():
        take(FAR_SIB[1], kof(2, 1, 1), q)

    def item(b2, dc):
        dz = jnp.where(b2 < 2, 0, jnp.where(b2 >= 6, 2, jnp.where(b2 % 2 == 0, 3, 1)))
        dh = jnp.where(b2 < 2, b2, jnp.where(b2 < 4, 0, jnp.where(b2 < 6, 1, b2 - 6)))
        return kof(dz, dh, dc)

    def amat(k, a):
        u = uc[k // 4, k % 4]
        xk = xb[k].astype(f32)
        for sh in range(2):
            xm = xk[:, sh * 8 : sh * 8 + 8, :].reshape(64, 128).astype(bf16)
            both = dot(u, xm, TN).astype(bf16)
            a[2 * sh] = both[:, :64]
            a[2 * sh + 1] = both[:, 64:]

    def pmat(k, a, p, b):
        n = slice(b * 256, b * 256 + 256)
        wb = w_ref[:, n].astype(f32)
        for s in range(4):
            p[s, :, n] = (dot(a[s], uv[k, b], NN) * wb).astype(bf16)

    def partner(kp):
        k = jnp.int32(0)
        for i in range(1, 16):
            k = jnp.where(tab_ref[i, q] == kp, i, k)
        return k

    def gmat(u, kp, p, b):
        n = slice(b * 256, b * 256 + 256)
        for s in range(4):
            g[kp, s * 64 : s * 64 + 64, n] = dot(u, p[s, :, n], NN).astype(bf16)

    def half(b2, dc, b2n, dcn, pr, pw, an):
        kp, kn = item(b2, dc), item(b2n, dcn)
        kk = partner(kp)
        u = uc[kk // 4, kk % 4]
        amat(kn, an)
        for b in range(8):
            gmat(u, kp, pr, b)
            pmat(kn, an, pw, b)

    def gmat_all(b2, dc, p):
        kp = item(b2, dc)
        kk = partner(kp)
        u = uc[kk // 4, kk % 4]
        for b in range(8):
            gmat(u, kp, p, b)

    def pmat_all(b2, dc, a, p):
        k = item(b2, dc)
        amat(k, a)
        for b in range(8):
            pmat(k, a, p, b)

    for j in (6, 5, 7, 4, 2, 1, 3):
        for copy in tcopy(j, t, at_offset(j, 1)):
            copy.start()
    for dz, dh in away:
        ccopy(dz * 2 + dh, 0, 0, 0, kof(dz, dh, 0)).start()
    ccopy(8, 0, 0, 0, sib).start()
    for j in range(1, 4):
        for copy in tcopy(j, at_offset(j, -1), t):
            copy.wait_recv()
    send_own(0)
    for j in range(4, 8):
        for copy in tcopy(j, at_offset(j, -1), t):
            copy.wait_recv()
    send_own(1)
    local[3].wait()
    local[4].wait()
    pmat_all(0, 0, a0, p0)
    for dz, dh in away:
        ccopy((4 - dz) % 4 * 2 + dh, dz, dh, 0, q).wait_recv()
        ccopy(8 + dz * 2 + dh, dz, dh, 0, sib).start()
    x_item(0)
    for i in range(2):
        take(OWN_SIB[i], kof(0, 0, 1), q, part(i))
    ccopy(8, 0, 0, 1, q).wait_recv()
    pmat_all(0, 1, a1, p1)
    for dz, dh in away:
        ccopy(8 + dz * 2 + dh, dz, dh, 1, q).wait_recv()
    gmat_all(0, 0, p0)
    x_item(1)
    gmat_all(0, 1, p1)
    pass_on(0, OWN_UP, OWN_DN)
    pmat_all(1, 0, a0, p0)

    odd = {3: boundary_3, 5: boundary_5, 7: boundary_7, 9: boundary_9, 11: boundary_11, 13: boundary_13}
    even = {6: boundary_6, 8: boundary_8, 10: boundary_10}

    def body(j, carry):
        for b, act in odd.items():
            pl.when(2 * j + 3 == b)(act)
        half(j + 1, 0, j + 1, 1, p0, p1, a1)
        for b, act in even.items():
            pl.when(2 * j + 4 == b)(act)
        half(j + 1, 1, j + 2, 0, p1, p0, a0)
        return carry

    lax.fori_loop(0, 6, body, 0)
    boundary_15()
    half(7, 0, 7, 1, p0, p1, a1)
    gmat_all(7, 1, p1)

    def ymat(k):
        kp = tab_ref[k, q]
        acc = jnp.zeros((256, 64), f32)
        for b in range(8):
            acc = acc + dot(g[kp, :, b * 256 : b * 256 + 256], uv[k, b], NT)
        both = jnp.concatenate([acc[:128], acc[128:]], axis=1)
        return jnp.swapaxes(both.reshape(2, 8, 8, 128), 0, 1).reshape(8, 16, 128)

    chip = q // 2

    def scopy(m):
        return remote(ysout.at[m], ysin.at[m], ssend.at[m], srecv.at[m], sib, t)

    def to_sibling(j, carry):
        pair = [(chip + 2 * j + i) % 8 for i in range(2)]
        for m, part_sum in [(m, ymat(m * 2 + 1 - c)) for m in pair]:
            ysout[m] = part_sum.astype(bf16)
        for m in pair:
            scopy(m).start()
        return carry

    lax.fori_loop(0, 4, to_sibling, 0)

    def ycopy(j, m, owner, peer):
        return remote(yout.at[m, peer], yin.at[chip, owner], ysend.at[j], yrecv.at[j], m * 2 + c, peer)

    own = pltpu.make_async_copy(yout.at[chip, t], yin.at[chip, t], yrecv.at[0])

    def to_owners(j, carry):
        pair = [(chip + 2 * j + i) % 8 for i in (1, 2)]
        sums = [ymat(m * 2 + c) for m in pair]
        for m in pair:
            scopy(m).wait_recv()
        for m, part_sum in zip(pair, sums):
            yout[m] = (part_sum + ysin[m].astype(f32)).astype(bf16)
        for off, m in enumerate(pair):
            for i in range(8):
                ycopy(2 * j + 1 + off, m, t, (t + i) % 8).start()
        return carry

    lax.fori_loop(0, 3, to_owners, 0)
    sums = [ymat((chip + 7) % 8 * 2 + c), ymat(q)]
    for m, part_sum in zip(((chip + 7) % 8, chip), sums):
        scopy(m).wait_recv()
        yout[m] = (part_sum + ysin[m].astype(f32)).astype(bf16)
    for i in range(8):
        ycopy(7, (chip + 7) % 8, t, (t + i) % 8).start()
    for i in range(1, 8):
        ycopy(0, chip, t, (t + i) % 8).start()
    own.start()

    res = jnp.zeros((16, 128), f32)
    for j in (1, 2, 3, 4, 5, 6, 7, 0):
        m = (chip - j + 8) % 8
        pltpu.make_async_copy(yin.at[m], yin.at[m], yrecv.at[j]).wait()
        res = res + jnp.sum(yin[m].astype(f32), axis=0)
    for s in range(4):
        for b in range(8):
            os[s : s + 1, b * 64 : b * 64 + 64] = res[
                (s % 2) * 8 + b : (s % 2) * 8 + b + 1, (s // 2) * 64 : (s // 2) * 64 + 64
            ]
    out_ref[0] = os[...].astype(bf16)

    for j in range(1, 8):
        for copy in tcopy(j, t, at_offset(j, 1)):
            copy.wait_send()
        pltpu.make_async_copy(yout.at[j], yout.at[j], ysend.at[j]).wait()
    pltpu.make_async_copy(yout.at[0, pl.ds(0, 7)], yout.at[0, pl.ds(0, 7)], ysend.at[0]).wait()
    for j in range(8):
        scopy(j).wait_send()
    for j in range(1, 16):
        ccopy(j, 0, 0, 0, sib).wait_send()
    for kind in range(KINDS):
        for copy in record(kind, me, sib, None if kind in WHOLE else 0):
            copy.wait_send()


def shards(trials, w_screen, cond_bands, val_bands, pair_table):
    vmem = pl.BlockSpec(memory_space=pltpu.VMEM)
    hbm = pl.BlockSpec(memory_space=pltpu.HBM)
    dma = pltpu.SemaphoreType.DMA
    return pl.pallas_call(
        kernel,
        out_shape=jax.ShapeDtypeStruct(trials.shape, bf16),
        in_specs=[hbm] * 5,
        out_specs=vmem,
        scratch_shapes=[
            pltpu.VMEM((4, 512), bf16),
            pltpu.VMEM((256, 2048), bf16),
            pltpu.SMEM((16, 16), jnp.int32),
            pltpu.VMEM((16, 8, 64, 256), bf16),
            pltpu.VMEM((16, 8, 16, 128), bf16),
            pltpu.VMEM((4, 4, 64, 256), bf16),
            pltpu.VMEM((4, 256, 2048), bf16),
            pltpu.VMEM((4, 256, 2048), bf16),
            pltpu.VMEM((4, 256, 64), bf16),
            pltpu.VMEM((4, 256, 64), bf16),
            pltpu.VMEM((16, 256, 2048), bf16),
            pltpu.VMEM((8, 8, 16, 128), bf16),
            pltpu.VMEM((8, 8, 16, 128), bf16),
            pltpu.VMEM((8, 8, 16, 128), bf16),
            pltpu.VMEM((8, 8, 16, 128), bf16),
            pltpu.VMEM((16, 128), f32),
            pltpu.VMEM((4, 512), f32),
            dma((5,)),
            dma((2, 8)), dma((2, 8)),
            dma((16,)), dma((16,)),
            dma((2, KINDS)), dma((2, KINDS)),
            dma((8,)), dma((8,)),
            dma((8,)), dma((8,)),
        ],
        compiler_params=pltpu.CompilerParams(
            collective_id=0, has_side_effects=True, vmem_limit_bytes=VMEM_LIMIT
        ),
    )(trials, w_screen, jnp.swapaxes(cond_bands, 1, 2), jnp.swapaxes(val_bands, 1, 2), pair_table)


def solution(mesh):
    in_specs = (
        P("pb", None, "tile"),
        P("pb", "tile", None),
        P("pb", "tile", None),
        P("pb", "tile", None),
        P(),
    )
    out_specs = P("pb", None, "tile")
    return jax.shard_map(shards, mesh=mesh, in_specs=in_specs, out_specs=out_specs, check_vma=False)
```

```python
import jax
import jax.numpy as jnp
from jax import lax
from jax.experimental import pallas as pl
from jax.experimental.pallas import tpu as pltpu
from jax.sharding import PartitionSpec as P

MESH = pl.DeviceIdType.MESH
bf16 = jnp.bfloat16
f32 = jnp.float32
f8 = jnp.float8_e4m3fn
TINY = 2.0**-100
NN = (((1,), (0,)), ((), ()))
NT = (((1,), (1,)), ((), ()))
TN = (((0,), (0,)), ((), ()))

OWN_X, OWN_UP, OWN_DN, OWN_SIB = (0, 1), (2, 3), (4, 5), (6, 7)
XC_UP, XC_DN, XC_SIB = (8, 9), (10, 11), (12, 13)
FAR_UP, FAR_DN = (14, 15), (16, 17)
DN_SIB, UP_SIB, FAR_SIB = (18, 19), (20, 21), (22, 23)
KINDS = 24
VMEM_LIMIT = 60 * 2**20
WHOLE = (18, 19, 20, 21, 22, 23)


def dot(a, b, dims):
    return lax.dot_general(a, b, dims, preferred_element_type=f32)


def kernel(
    x_hbm, w_hbm, uc_hbm, uv_hbm, tab_hbm, out_ref,
    x_ref, w_ref, tab_ref, uv, xb, uc, p0, p1, a0, a1, e0, e1, g, ysout, ysin, yout, yin, xs, os,
    lsem, tsend, trecv, ucsend, ucrecv, isend, irecv, ssend, srecv, ysend, yrecv,
):
    q = lax.axis_index("pb")
    t = lax.axis_index("tile")
    z, h, c = q // 4, (q // 2) % 2, q % 2
    hi, y = t // 4, t % 4

    def kof(dz, dh, dc):
        return ((z + dz) % 4) * 4 + ((h + dh) % 2) * 2 + (c + dc) % 2

    me = kof(0, 0, 0)
    local = (
        pltpu.make_async_copy(x_hbm.at[0], x_ref, lsem.at[0]),
        pltpu.make_async_copy(uv_hbm.at[0], uv.at[me, t], lsem.at[1]),
        pltpu.make_async_copy(uc_hbm.at[0], uc.at[z, q % 4], lsem.at[2]),
        pltpu.make_async_copy(w_hbm.at[0], w_ref, lsem.at[3]),
        pltpu.make_async_copy(tab_hbm, tab_ref, lsem.at[4]),
    )
    for copy in local:
        copy.start()

    barrier = pltpu.get_barrier_semaphore()
    for j in range(1, 8):
        pl.semaphore_signal(barrier, inc=1, device_id=(q, (t + j) % 8), device_id_type=MESH)
    for j in range(1, 16):
        pl.semaphore_signal(barrier, inc=1, device_id=((q + j) % 16, t), device_id_type=MESH)

    local[0].wait()
    xin = x_ref[...].astype(f32)
    for s in range(4):
        for b in range(8):
            xs[(s // 2) * 8 + b : (s // 2) * 8 + b + 1, (s % 2) * 64 : (s % 2) * 64 + 64] = xin[
                s : s + 1, b * 64 : b * 64 + 64
            ]
    xb[me, t] = xs[...].astype(bf16)
    local[1].wait()
    local[2].wait()

    pl.semaphore_wait(barrier, 22)

    def remote(src, dst, ssem, rsem, pb, tile):
        return pltpu.make_async_remote_copy(
            src_ref=src, dst_ref=dst, send_sem=ssem, recv_sem=rsem,
            device_id=(pb, tile), device_id_type=MESH,
        )

    def at_offset(j, sign):
        return ((hi + j // 4) % 2) * 4 + (y + sign * (j % 4) + 4) % 4

    def tcopy(j, owner, peer):
        return (
            remote(xb.at[me, owner], xb.at[me, owner], tsend.at[1, j], trecv.at[1, j], q, peer),
            remote(uv.at[me, owner], uv.at[me, owner], tsend.at[0, j], trecv.at[0, j], q, peer),
        )

    def ccopy(kind, dz, dh, dc, peer):
        blk = uc.at[(z + dz) % 4, kof(0, dh, dc) % 4]
        return remote(blk, blk, ucsend.at[kind], ucrecv.at[kind], peer, t)

    sib, xnb, up, dn = kof(0, 0, 1), kof(0, 1, 0), kof(1, 0, 0), kof(3, 0, 0)

    away = ((2, 1), (2, 0), (1, 1), (3, 1), (1, 0), (3, 0), (0, 1))

    def record(kind, k, peer, first=None):
        at = (k,) if first is None else (k, pl.ds(first * 4, 4))
        return (
            remote(xb.at[at], xb.at[at], isend.at[1, kind], irecv.at[1, kind], peer, t),
            remote(uv.at[at], uv.at[at], isend.at[0, kind], irecv.at[0, kind], peer, t),
        )

    def send(*args):
        for copy in record(*args):
            copy.start()

    def take(*args):
        for copy in record(*args):
            copy.wait_recv()

    def part(i):
        return (hi + i) % 2

    def send_own(i):
        send(OWN_X[i], me, xnb, part(i))
        send(OWN_UP[i], me, up, part(i))
        send(OWN_DN[i], me, dn, part(i))
        send(OWN_SIB[i], me, sib, part(i))

    def x_item(i):
        k = kof(0, 1, 0)
        take(OWN_X[i], k, q, part(i))
        send(XC_UP[i], k, up, part(i))
        send(XC_DN[i], k, dn, part(i))
        send(XC_SIB[i], k, sib, part(i))

    def pass_on(dh, from_dn, from_up):
        k = kof(3, dh, 0)
        for i in range(2):
            take(from_dn[i], k, q, part(i))
        send(FAR_UP[dh], k, up, 0)
        send(DN_SIB[dh], k, sib)
        k = kof(1, dh, 0)
        for i in range(2):
            take(from_up[i], k, q, part(i))
        send(FAR_DN[dh], k, dn, 1)
        send(UP_SIB[dh], k, sib)

    def boundary_3():
        for i in range(2):
            take(XC_SIB[i], kof(0, 1, 1), q, part(i))

    def far(dh):
        k = kof(2, dh, 0)
        take(FAR_UP[dh], k, q, 0)
        take(FAR_DN[dh], k, q, 1)
        send(FAR_SIB[dh], k, sib)

    def boundary_4():
        take(DN_SIB[0], kof(3, 0, 1), q)

    def boundary_6():
        pass_on(1, XC_UP, XC_DN)
        take(UP_SIB[0], kof(1, 0, 1), q)

    def boundary_8():
        far(0)
        take(DN_SIB[1], kof(3, 1, 1), q)

    def boundary_10():
        far(1)
        take(UP_SIB[1], kof(1, 1, 1), q)

    def boundary_12():
        take(FAR_SIB[0], kof(2, 0, 1), q)

    def boundary_14():
        take(FAR_SIB[1], kof(2, 1, 1), q)

    def item(b2, dc):
        dz = jnp.where(b2 < 2, 0, jnp.where(b2 >= 6, 2, jnp.where(b2 % 2 == 0, 3, 1)))
        dh = jnp.where(b2 < 2, b2, jnp.where(b2 < 4, 0, jnp.where(b2 < 6, 1, b2 - 6)))
        return kof(dz, dh, dc)

    lane = lax.broadcasted_iota(jnp.int32, (64, 128), 1)
    column = lax.broadcasted_iota(jnp.int32, (256, 128), 1)

    def level(top):
        return jnp.floor(jnp.log2(jnp.maximum(top, TINY)))

    def split(value):
        hi = value.astype(f8)
        return hi, (value - hi.astype(f32)).astype(f8)

    def amat(k, a, back):
        u = jnp.transpose(uc[k // 4, k % 4].astype(f32)).astype(bf16)
        xk = xb[k].astype(f32)
        tops = jnp.zeros((256, 128), f32)
        values = []
        for sh in range(2):
            xm = xk[:, sh * 8 : sh * 8 + 8, :].reshape(64, 128)
            xr = pltpu.roll(xm, 64, 1)
            twice = [jnp.where((lane < 64) == (sl == 0), xm, xr).astype(bf16) for sl in range(2)]
            both = dot(u, jnp.concatenate(twice, axis=1), NN).astype(bf16).astype(f32)
            for sl in range(2):
                av = both[:, sl * 128 : sl * 128 + 128]
                top = jnp.max(jnp.abs(av), axis=1, keepdims=True)
                tops = jnp.where(column == 2 * sh + sl, top, tops)
                values.append(av)
        levels = level(tops)
        scale = jnp.exp2(7.0 - levels)
        for s, av in enumerate(values):
            hi, lo = split(av * scale[:, s : s + 1])
            a[s, :, :128] = hi
            a[s, :, 128:] = lo
        back[...] = jnp.exp2(jnp.transpose(levels)[:8] - 7.0)

    def pmat(k, a, p, b):
        n = slice(b * 256, b * 256 + 256)
        ub = uv[k, b].astype(f32)
        lev = level(jnp.max(jnp.abs(ub), axis=0, keepdims=True))
        hi, lo = split(ub * jnp.exp2(7.0 - lev))
        u8 = jnp.concatenate([hi, lo, hi, lo], axis=0)
        wb = w_ref[:, n].astype(f32) * jnp.exp2(lev - 7.0)
        for s in range(4):
            p[s, :, n] = (dot(a[s], u8, NN) * wb).astype(bf16)

    def partner(kp):
        k = jnp.int32(0)
        for i in range(1, 16):
            k = jnp.where(tab_ref[i, q] == kp, i, k)
        return k

    def scaled(kp, back):
        kk = partner(kp)
        u = uc[kk // 4, kk % 4].astype(f32)
        return [(u * back[s : s + 1, :]).astype(bf16) for s in range(4)]

    def gmat(us, kp, p, b):
        n = slice(b * 256, b * 256 + 256)
        for s in range(4):
            g[kp, s * 64 : s * 64 + 64, n] = dot(us[s], p[s, :, n], NN).astype(bf16)

    def half(g_item, m_item, a_item, pr, pw, am, aw, back):
        us = scaled(g_item, back)
        for b in range(8):
            gmat(us, g_item, pr, b)
            pmat(m_item, am, pw, b)
            if b == 3 and a_item is not None:
                amat(a_item, aw, back)

    def gmat_all(b2, dc, p, back):
        kp = item(b2, dc)
        us = scaled(kp, back)
        for b in range(8):
            gmat(us, kp, p, b)

    def pmat_all(b2, dc, a, p, back):
        k = item(b2, dc)
        amat(k, a, back)
        for b in range(8):
            pmat(k, a, p, b)

    for j in (6, 5, 7, 4, 2, 1, 3):
        for copy in tcopy(j, t, at_offset(j, 1)):
            copy.start()
    for dz, dh in away:
        ccopy(dz * 2 + dh, 0, 0, 0, kof(dz, dh, 0)).start()
    ccopy(8, 0, 0, 0, sib).start()
    for j in range(1, 4):
        for copy in tcopy(j, at_offset(j, -1), t):
            copy.wait_recv()
    send_own(0)
    for j in range(4, 8):
        for copy in tcopy(j, at_offset(j, -1), t):
            copy.wait_recv()
    send_own(1)
    local[3].wait()
    local[4].wait()
    pmat_all(0, 0, a0, p0, e0)
    for dz, dh in away:
        ccopy((4 - dz) % 4 * 2 + dh, dz, dh, 0, q).wait_recv()
        ccopy(8 + dz * 2 + dh, dz, dh, 0, sib).start()
    for i in range(2):
        take(OWN_SIB[i], kof(0, 0, 1), q, part(i))
    ccopy(8, 0, 0, 1, q).wait_recv()
    pmat_all(0, 1, a1, p1, e1)
    x_item(0)
    for dz, dh in away:
        ccopy(8 + dz * 2 + dh, dz, dh, 1, q).wait_recv()
    gmat_all(0, 0, p0, e0)
    x_item(1)
    gmat_all(0, 1, p1, e1)
    pmat_all(1, 0, a0, p0, e0)
    pass_on(0, OWN_UP, OWN_DN)

    boundary_3()
    amat(item(1, 1), a1, e1)
    acts = {4: boundary_4, 6: boundary_6, 8: boundary_8, 10: boundary_10, 12: boundary_12, 14: boundary_14}

    def body(j, carry):
        half(item(j + 1, 0), item(j + 1, 1), item(j + 2, 0), p0, p1, a1, a0, e0)
        for b, act in acts.items():
            pl.when(2 * j + 4 == b)(act)
        half(item(j + 1, 1), item(j + 2, 0), item(j + 2, 1), p1, p0, a0, a1, e1)
        return carry

    lax.fori_loop(0, 6, body, 0)
    half(item(7, 0), item(7, 1), None, p0, p1, a1, a0, e0)
    gmat_all(7, 1, p1, e1)

    def ymat(k):
        kp = tab_ref[k, q]
        acc = jnp.zeros((256, 64), f32)
        for b in range(8):
            acc = acc + dot(g[kp, :, b * 256 : b * 256 + 256], uv[k, b], NT)
        both = jnp.concatenate([acc[:128], acc[128:]], axis=1)
        return jnp.swapaxes(both.reshape(2, 8, 8, 128), 0, 1).reshape(8, 16, 128)

    chip = q // 2

    def scopy(m):
        return remote(ysout.at[m], ysin.at[m], ssend.at[m], srecv.at[m], sib, t)

    def to_sibling(j, carry):
        pair = [(chip + 2 * j + i) % 8 for i in range(2)]
        for m, part_sum in [(m, ymat(m * 2 + 1 - c)) for m in pair]:
            ysout[m] = part_sum.astype(bf16)
        for m in pair:
            scopy(m).start()
        return carry

    lax.fori_loop(0, 4, to_sibling, 0)

    def ycopy(j, m, owner, peer):
        return remote(yout.at[m, peer], yin.at[chip, owner], ysend.at[j], yrecv.at[j], m * 2 + c, peer)

    own = pltpu.make_async_copy(yout.at[chip, t], yin.at[chip, t], yrecv.at[0])

    def to_owners(j, carry):
        pair = [(chip + 2 * j + i) % 8 for i in (1, 2)]
        sums = [ymat(m * 2 + c) for m in pair]
        for m in pair:
            scopy(m).wait_recv()
        for m, part_sum in zip(pair, sums):
            yout[m] = (part_sum + ysin[m].astype(f32)).astype(bf16)
        for off, m in enumerate(pair):
            for i in range(8):
                ycopy(2 * j + 1 + off, m, t, (t + i) % 8).start()
        return carry

    lax.fori_loop(0, 3, to_owners, 0)
    sums = [ymat((chip + 7) % 8 * 2 + c), ymat(q)]
    for m, part_sum in zip(((chip + 7) % 8, chip), sums):
        scopy(m).wait_recv()
        yout[m] = (part_sum + ysin[m].astype(f32)).astype(bf16)
    for i in range(8):
        ycopy(7, (chip + 7) % 8, t, (t + i) % 8).start()
    for i in range(1, 8):
        ycopy(0, chip, t, (t + i) % 8).start()
    own.start()

    res = jnp.zeros((16, 128), f32)
    for j in (1, 2, 3, 4, 5, 6, 7, 0):
        m = (chip - j + 8) % 8
        pltpu.make_async_copy(yin.at[m], yin.at[m], yrecv.at[j]).wait()
        res = res + jnp.sum(yin[m].astype(f32), axis=0)
    for s in range(4):
        for b in range(8):
            os[s : s + 1, b * 64 : b * 64 + 64] = res[
                (s % 2) * 8 + b : (s % 2) * 8 + b + 1, (s // 2) * 64 : (s // 2) * 64 + 64
            ]
    out_ref[0] = os[...].astype(bf16)

    for j in range(1, 8):
        for copy in tcopy(j, t, at_offset(j, 1)):
            copy.wait_send()
        pltpu.make_async_copy(yout.at[j], yout.at[j], ysend.at[j]).wait()
    pltpu.make_async_copy(yout.at[0, pl.ds(0, 7)], yout.at[0, pl.ds(0, 7)], ysend.at[0]).wait()
    for j in range(8):
        scopy(j).wait_send()
    for j in range(1, 16):
        ccopy(j, 0, 0, 0, sib).wait_send()
    for kind in range(KINDS):
        for copy in record(kind, me, sib, None if kind in WHOLE else 0):
            copy.wait_send()


def shards(trials, w_screen, cond_bands, val_bands, pair_table):
    vmem = pl.BlockSpec(memory_space=pltpu.VMEM)
    hbm = pl.BlockSpec(memory_space=pltpu.HBM)
    dma = pltpu.SemaphoreType.DMA
    return pl.pallas_call(
        kernel,
        out_shape=jax.ShapeDtypeStruct(trials.shape, bf16),
        in_specs=[hbm] * 5,
        out_specs=vmem,
        scratch_shapes=[
            pltpu.VMEM((4, 512), bf16),
            pltpu.VMEM((256, 2048), bf16),
            pltpu.SMEM((16, 16), jnp.int32),
            pltpu.VMEM((16, 8, 64, 256), bf16),
            pltpu.VMEM((16, 8, 16, 128), bf16),
            pltpu.VMEM((4, 4, 64, 256), bf16),
            pltpu.VMEM((4, 256, 2048), bf16),
            pltpu.VMEM((4, 256, 2048), bf16),
            pltpu.VMEM((4, 256, 256), f8),
            pltpu.VMEM((4, 256, 256), f8),
            pltpu.VMEM((8, 256), f32),
            pltpu.VMEM((8, 256), f32),
            pltpu.VMEM((16, 256, 2048), bf16),
            pltpu.VMEM((8, 8, 16, 128), bf16),
            pltpu.VMEM((8, 8, 16, 128), bf16),
            pltpu.VMEM((8, 8, 16, 128), bf16),
            pltpu.VMEM((8, 8, 16, 128), bf16),
            pltpu.VMEM((16, 128), f32),
            pltpu.VMEM((4, 512), f32),
            dma((5,)),
            dma((2, 8)), dma((2, 8)),
            dma((16,)), dma((16,)),
            dma((2, KINDS)), dma((2, KINDS)),
            dma((8,)), dma((8,)),
            dma((8,)), dma((8,)),
        ],
        compiler_params=pltpu.CompilerParams(
            collective_id=0, has_side_effects=True, vmem_limit_bytes=VMEM_LIMIT
        ),
    )(trials, w_screen, jnp.swapaxes(cond_bands, 1, 2), jnp.swapaxes(val_bands, 1, 2), pair_table)


def solution(mesh):
    in_specs = (
        P("pb", None, "tile"),
        P("pb", "tile", None),
        P("pb", "tile", None),
        P("pb", "tile", None),
        P(),
    )
    out_specs = P("pb", None, "tile")
    return jax.shard_map(shards, mesh=mesh, in_specs=in_specs, out_specs=out_specs, check_vma=False)
```

```python
import jax
import jax.numpy as jnp
from jax import lax
from jax.experimental import pallas as pl
from jax.experimental.pallas import tpu as pltpu
from jax.sharding import PartitionSpec as P

MESH = pl.DeviceIdType.MESH
bf16 = jnp.bfloat16
f32 = jnp.float32
f8 = jnp.float8_e4m3fn
TINY = 2.0**-100
NN = (((1,), (0,)), ((), ()))
NT = (((1,), (1,)), ((), ()))
TN = (((0,), (0,)), ((), ()))

OWN_X, OWN_UP, OWN_DN, OWN_SIB = (0, 1), (2, 3), (4, 5), (6, 7)
XC_UP, XC_DN, XC_SIB = (8, 9), (10, 11), (12, 13)
FAR_UP, FAR_DN = (14, 15), (16, 17)
DN_SIB, UP_SIB, FAR_SIB = (18, 19), (20, 21), (22, 23)
KINDS = 24
VMEM_LIMIT = 60 * 2**20
WHOLE = (18, 19, 20, 21, 22, 23)


def dot(a, b, dims):
    return lax.dot_general(a, b, dims, preferred_element_type=f32)


def kernel(
    x_hbm, w_hbm, uc_hbm, uv_hbm, tab_hbm, out_ref,
    x_ref, w_ref, tab_ref, uv, xb, uc, p0, p1, a0, a1, e0, e1, g, ysout, ysin, yout, yin, xs, os,
    lsem, tsend, trecv, ucsend, ucrecv, isend, irecv, ssend, srecv, ysend, yrecv,
):
    q = lax.axis_index("pb")
    t = lax.axis_index("tile")
    z, h, c = q // 4, (q // 2) % 2, q % 2
    hi, y = t // 4, t % 4

    def kof(dz, dh, dc):
        return ((z + dz) % 4) * 4 + ((h + dh) % 2) * 2 + (c + dc) % 2

    me = kof(0, 0, 0)
    local = (
        pltpu.make_async_copy(x_hbm.at[0], x_ref, lsem.at[0]),
        pltpu.make_async_copy(uv_hbm.at[0], uv.at[me, t], lsem.at[1]),
        pltpu.make_async_copy(uc_hbm.at[0], uc.at[z, q % 4], lsem.at[2]),
        pltpu.make_async_copy(w_hbm.at[0], w_ref, lsem.at[3]),
        pltpu.make_async_copy(tab_hbm, tab_ref, lsem.at[4]),
    )
    for copy in local:
        copy.start()

    barrier = pltpu.get_barrier_semaphore()
    for j in range(1, 8):
        pl.semaphore_signal(barrier, inc=1, device_id=(q, (t + j) % 8), device_id_type=MESH)
    for j in range(1, 16):
        pl.semaphore_signal(barrier, inc=1, device_id=((q + j) % 16, t), device_id_type=MESH)

    local[0].wait()
    xin = x_ref[...].astype(f32)
    for s in range(4):
        for b in range(8):
            xs[(s // 2) * 8 + b : (s // 2) * 8 + b + 1, (s % 2) * 64 : (s % 2) * 64 + 64] = xin[
                s : s + 1, b * 64 : b * 64 + 64
            ]
    xb[me, t] = xs[...].astype(bf16)
    local[1].wait()
    local[2].wait()

    pl.semaphore_wait(barrier, 22)

    def remote(src, dst, ssem, rsem, pb, tile):
        return pltpu.make_async_remote_copy(
            src_ref=src, dst_ref=dst, send_sem=ssem, recv_sem=rsem,
            device_id=(pb, tile), device_id_type=MESH,
        )

    def at_offset(j, sign):
        return ((hi + j // 4) % 2) * 4 + (y + sign * (j % 4) + 4) % 4

    def tcopy(j, owner, peer):
        return (
            remote(xb.at[me, owner], xb.at[me, owner], tsend.at[1, j], trecv.at[1, j], q, peer),
            remote(uv.at[me, owner], uv.at[me, owner], tsend.at[0, j], trecv.at[0, j], q, peer),
        )

    def ccopy(kind, dz, dh, dc, peer):
        blk = uc.at[(z + dz) % 4, kof(0, dh, dc) % 4]
        return remote(blk, blk, ucsend.at[kind], ucrecv.at[kind], peer, t)

    sib, xnb, up, dn = kof(0, 0, 1), kof(0, 1, 0), kof(1, 0, 0), kof(3, 0, 0)

    away = ((2, 1), (2, 0), (1, 1), (3, 1), (1, 0), (3, 0), (0, 1))

    def record(kind, k, peer, first=None):
        at = (k,) if first is None else (k, pl.ds(first * 4, 4))
        return (
            remote(xb.at[at], xb.at[at], isend.at[1, kind], irecv.at[1, kind], peer, t),
            remote(uv.at[at], uv.at[at], isend.at[0, kind], irecv.at[0, kind], peer, t),
        )

    def send(*args):
        for copy in record(*args):
            copy.start()

    def take(*args):
        for copy in record(*args):
            copy.wait_recv()

    def part(i):
        return (hi + i) % 2

    def send_own(i):
        send(OWN_X[i], me, xnb, part(i))
        send(OWN_UP[i], me, up, part(i))
        send(OWN_DN[i], me, dn, part(i))
        send(OWN_SIB[i], me, sib, part(i))

    def x_item(i):
        k = kof(0, 1, 0)
        take(OWN_X[i], k, q, part(i))
        send(XC_UP[i], k, up, part(i))
        send(XC_DN[i], k, dn, part(i))
        send(XC_SIB[i], k, sib, part(i))

    def pass_on(dh, from_dn, from_up):
        k = kof(3, dh, 0)
        for i in range(2):
            take(from_dn[i], k, q, part(i))
        send(FAR_UP[dh], k, up, 0)
        send(DN_SIB[dh], k, sib)
        k = kof(1, dh, 0)
        for i in range(2):
            take(from_up[i], k, q, part(i))
        send(FAR_DN[dh], k, dn, 1)
        send(UP_SIB[dh], k, sib)

    def boundary_3():
        for i in range(2):
            take(XC_SIB[i], kof(0, 1, 1), q, part(i))

    def far(dh):
        k = kof(2, dh, 0)
        take(FAR_UP[dh], k, q, 0)
        take(FAR_DN[dh], k, q, 1)
        send(FAR_SIB[dh], k, sib)

    def boundary_4():
        take(DN_SIB[0], kof(3, 0, 1), q)

    def boundary_6():
        pass_on(1, XC_UP, XC_DN)
        take(UP_SIB[0], kof(1, 0, 1), q)

    def boundary_8():
        far(0)
        take(DN_SIB[1], kof(3, 1, 1), q)

    def boundary_10():
        far(1)
        take(UP_SIB[1], kof(1, 1, 1), q)

    def boundary_12():
        take(FAR_SIB[0], kof(2, 0, 1), q)

    def boundary_14():
        take(FAR_SIB[1], kof(2, 1, 1), q)

    def item(b2, dc):
        dz = jnp.where(b2 < 2, 0, jnp.where(b2 >= 6, 2, jnp.where(b2 % 2 == 0, 3, 1)))
        dh = jnp.where(b2 < 2, b2, jnp.where(b2 < 4, 0, jnp.where(b2 < 6, 1, b2 - 6)))
        return kof(dz, dh, dc)

    lane = lax.broadcasted_iota(jnp.int32, (64, 128), 1)
    column = lax.broadcasted_iota(jnp.int32, (256, 128), 1)

    def level(top):
        return jnp.floor(jnp.log2(jnp.maximum(top, TINY)))

    def split(value):
        hi = value.astype(f8)
        return hi, (value - hi.astype(f32)).astype(f8)

    def amat_parts(k, a, back):
        u = jnp.transpose(uc[k // 4, k % 4].astype(f32)).astype(bf16)
        xk = xb[k].astype(f32)
        levels = jnp.zeros((256, 128), f32)
        for s in range(4):
            xm = xk[:, s // 2 * 8 : s // 2 * 8 + 8, :].reshape(64, 128)
            twice = jnp.where((lane < 64) == (s % 2 == 0), xm, pltpu.roll(xm, 64, 1)).astype(bf16)
            av = dot(u, twice, NN).astype(bf16).astype(f32)
            lev = level(jnp.max(jnp.abs(av), axis=1, keepdims=True))
            levels = jnp.where(column == s, lev, levels)
            hi, lo = split(av * jnp.exp2(7.0 - lev))
            a[s, :, :128] = hi
            a[s, :, 128:] = lo
            if s == 3:
                back[...] = jnp.exp2(jnp.transpose(levels)[:8] - 7.0)
            yield

    def amat(k, a, back):
        for _ in amat_parts(k, a, back):
            pass

    def pmat(k, a, p, b):
        n = slice(b * 256, b * 256 + 256)
        ub = uv[k, b].astype(f32)
        lev = level(jnp.max(jnp.abs(ub), axis=0, keepdims=True))
        hi, lo = split(ub * jnp.exp2(7.0 - lev))
        u8 = jnp.concatenate([hi, lo, hi, lo], axis=0)
        wb = w_ref[:, n].astype(f32) * jnp.exp2(lev - 7.0)
        for s in range(4):
            p[s, :, n] = (dot(a[s], u8, NN) * wb).astype(bf16)

    def partner(kp):
        k = jnp.int32(0)
        for i in range(1, 16):
            k = jnp.where(tab_ref[i, q] == kp, i, k)
        return k

    def scaled(kp, back):
        kk = partner(kp)
        u = uc[kk // 4, kk % 4].astype(f32)
        return [(u * back[s : s + 1, :]).astype(bf16) for s in range(4)]

    def gmat(us, kp, p, b):
        n = slice(b * 256, b * 256 + 256)
        for s in range(4):
            g[kp, s * 64 : s * 64 + 64, n] = dot(us[s], p[s, :, n], NN).astype(bf16)

    def half(g_item, m_item, a_item, pr, pw, am, aw, back):
        us = scaled(g_item, back)
        parts = iter(()) if a_item is None else amat_parts(a_item, aw, back)
        for b in range(8):
            gmat(us, g_item, pr, b)
            pmat(m_item, am, pw, b)
            if b % 2 == 0:
                next(parts, None)

    def gmat_all(b2, dc, p, back):
        kp = item(b2, dc)
        us = scaled(kp, back)
        for b in range(8):
            gmat(us, kp, p, b)

    def pmat_all(b2, dc, a, p, back):
        k = item(b2, dc)
        amat(k, a, back)
        for b in range(8):
            pmat(k, a, p, b)

    for j in (6, 5, 7, 4, 2, 1, 3):
        for copy in tcopy(j, t, at_offset(j, 1)):
            copy.start()
    for dz, dh in away:
        ccopy(dz * 2 + dh, 0, 0, 0, kof(dz, dh, 0)).start()
    ccopy(8, 0, 0, 0, sib).start()
    for j in range(1, 4):
        for copy in tcopy(j, at_offset(j, -1), t):
            copy.wait_recv()
    send_own(0)
    for j in range(4, 8):
        for copy in tcopy(j, at_offset(j, -1), t):
            copy.wait_recv()
    send_own(1)
    local[3].wait()
    local[4].wait()
    pmat_all(0, 0, a0, p0, e0)
    for dz, dh in away:
        ccopy((4 - dz) % 4 * 2 + dh, dz, dh, 0, q).wait_recv()
        ccopy(8 + dz * 2 + dh, dz, dh, 0, sib).start()
    for i in range(2):
        take(OWN_SIB[i], kof(0, 0, 1), q, part(i))
    ccopy(8, 0, 0, 1, q).wait_recv()
    pmat_all(0, 1, a1, p1, e1)
    x_item(0)
    for dz, dh in away:
        ccopy(8 + dz * 2 + dh, dz, dh, 1, q).wait_recv()
    gmat_all(0, 0, p0, e0)
    x_item(1)
    gmat_all(0, 1, p1, e1)
    pmat_all(1, 0, a0, p0, e0)
    pass_on(0, OWN_UP, OWN_DN)

    boundary_3()
    amat(item(1, 1), a1, e1)
    acts = {4: boundary_4, 6: boundary_6, 8: boundary_8, 10: boundary_10, 12: boundary_12, 14: boundary_14}

    def body(j, carry):
        half(item(j + 1, 0), item(j + 1, 1), item(j + 2, 0), p0, p1, a1, a0, e0)
        for b, act in acts.items():
            pl.when(2 * j + 4 == b)(act)
        half(item(j + 1, 1), item(j + 2, 0), item(j + 2, 1), p1, p0, a0, a1, e1)
        return carry

    lax.fori_loop(0, 6, body, 0)
    half(item(7, 0), item(7, 1), None, p0, p1, a1, a0, e0)
    gmat_all(7, 1, p1, e1)

    def ymat(k):
        kp = tab_ref[k, q]
        acc = jnp.zeros((256, 64), f32)
        for b in range(8):
            acc = acc + dot(g[kp, :, b * 256 : b * 256 + 256], uv[k, b], NT)
        both = jnp.concatenate([acc[:128], acc[128:]], axis=1)
        return jnp.swapaxes(both.reshape(2, 8, 8, 128), 0, 1).reshape(8, 16, 128)

    chip = q // 2

    def scopy(m):
        return remote(ysout.at[m], ysin.at[m], ssend.at[m], srecv.at[m], sib, t)

    def to_sibling(j, carry):
        pair = [(chip + 2 * j + i) % 8 for i in range(2)]
        for m, part_sum in [(m, ymat(m * 2 + 1 - c)) for m in pair]:
            ysout[m] = part_sum.astype(bf16)
        for m in pair:
            scopy(m).start()
        return carry

    lax.fori_loop(0, 4, to_sibling, 0)

    def ycopy(j, m, owner, peer):
        return remote(yout.at[m, peer], yin.at[chip, owner], ysend.at[j], yrecv.at[j], m * 2 + c, peer)

    own = pltpu.make_async_copy(yout.at[chip, t], yin.at[chip, t], yrecv.at[0])

    def to_owners(j, carry):
        pair = [(chip + 2 * j + i) % 8 for i in (1, 2)]
        sums = [ymat(m * 2 + c) for m in pair]
        for m in pair:
            scopy(m).wait_recv()
        for m, part_sum in zip(pair, sums):
            yout[m] = (part_sum + ysin[m].astype(f32)).astype(bf16)
        for off, m in enumerate(pair):
            for i in range(8):
                ycopy(2 * j + 1 + off, m, t, (t + i) % 8).start()
        return carry

    lax.fori_loop(0, 3, to_owners, 0)
    sums = [ymat((chip + 7) % 8 * 2 + c), ymat(q)]
    for m, part_sum in zip(((chip + 7) % 8, chip), sums):
        scopy(m).wait_recv()
        yout[m] = (part_sum + ysin[m].astype(f32)).astype(bf16)
    for i in range(8):
        ycopy(7, (chip + 7) % 8, t, (t + i) % 8).start()
    for i in range(1, 8):
        ycopy(0, chip, t, (t + i) % 8).start()
    own.start()

    res = jnp.zeros((16, 128), f32)
    for j in (1, 2, 3, 4, 5, 6, 7, 0):
        m = (chip - j + 8) % 8
        pltpu.make_async_copy(yin.at[m], yin.at[m], yrecv.at[j]).wait()
        res = res + jnp.sum(yin[m].astype(f32), axis=0)
    for s in range(4):
        for b in range(8):
            os[s : s + 1, b * 64 : b * 64 + 64] = res[
                (s % 2) * 8 + b : (s % 2) * 8 + b + 1, (s // 2) * 64 : (s // 2) * 64 + 64
            ]
    out_ref[0] = os[...].astype(bf16)

    for j in range(1, 8):
        for copy in tcopy(j, t, at_offset(j, 1)):
            copy.wait_send()
        pltpu.make_async_copy(yout.at[j], yout.at[j], ysend.at[j]).wait()
    pltpu.make_async_copy(yout.at[0, pl.ds(0, 7)], yout.at[0, pl.ds(0, 7)], ysend.at[0]).wait()
    for j in range(8):
        scopy(j).wait_send()
    for j in range(1, 16):
        ccopy(j, 0, 0, 0, sib).wait_send()
    for kind in range(KINDS):
        for copy in record(kind, me, sib, None if kind in WHOLE else 0):
            copy.wait_send()


def shards(trials, w_screen, cond_bands, val_bands, pair_table):
    vmem = pl.BlockSpec(memory_space=pltpu.VMEM)
    hbm = pl.BlockSpec(memory_space=pltpu.HBM)
    dma = pltpu.SemaphoreType.DMA
    return pl.pallas_call(
        kernel,
        out_shape=jax.ShapeDtypeStruct(trials.shape, bf16),
        in_specs=[hbm] * 5,
        out_specs=vmem,
        scratch_shapes=[
            pltpu.VMEM((4, 512), bf16),
            pltpu.VMEM((256, 2048), bf16),
            pltpu.SMEM((16, 16), jnp.int32),
            pltpu.VMEM((16, 8, 64, 256), bf16),
            pltpu.VMEM((16, 8, 16, 128), bf16),
            pltpu.VMEM((4, 4, 64, 256), bf16),
            pltpu.VMEM((4, 256, 2048), bf16),
            pltpu.VMEM((4, 256, 2048), bf16),
            pltpu.VMEM((4, 256, 256), f8),
            pltpu.VMEM((4, 256, 256), f8),
            pltpu.VMEM((8, 256), f32),
            pltpu.VMEM((8, 256), f32),
            pltpu.VMEM((16, 256, 2048), bf16),
            pltpu.VMEM((8, 8, 16, 128), bf16),
            pltpu.VMEM((8, 8, 16, 128), bf16),
            pltpu.VMEM((8, 8, 16, 128), bf16),
            pltpu.VMEM((8, 8, 16, 128), bf16),
            pltpu.VMEM((16, 128), f32),
            pltpu.VMEM((4, 512), f32),
            dma((5,)),
            dma((2, 8)), dma((2, 8)),
            dma((16,)), dma((16,)),
            dma((2, KINDS)), dma((2, KINDS)),
            dma((8,)), dma((8,)),
            dma((8,)), dma((8,)),
        ],
        compiler_params=pltpu.CompilerParams(
            collective_id=0, has_side_effects=True, vmem_limit_bytes=VMEM_LIMIT
        ),
    )(trials, w_screen, jnp.swapaxes(cond_bands, 1, 2), jnp.swapaxes(val_bands, 1, 2), pair_table)


def solution(mesh):
    in_specs = (
        P("pb", None, "tile"),
        P("pb", "tile", None),
        P("pb", "tile", None),
        P("pb", "tile", None),
        P(),
    )
    out_specs = P("pb", None, "tile")
    return jax.shard_map(shards, mesh=mesh, in_specs=in_specs, out_specs=out_specs, check_vma=False)
```
